256 devices in a mesh: instance: 4 (over y), sector: 32 (over x, z), radial: 2 (over core).
Axes of the slice: x: 4, y: 4, z: 8, core: 2. Of those that a mesh axis runs over, the one named last changes fastest.
Arguments:
- flow_state: float32 [8, 3, 5, 128, 8192], P('instance', None, None, 'radial', 'sector'), may hold values from -6 to 6
- rotor_face: float32 [8, 2, 5, 128, 8192], P('instance', None, None, 'radial', 'sector'), may hold values from -6 to 6
- jacobians: float32 [3, 5, 5], replicated, may hold values from -2.5 to 2.5
- rotor_shift: int32 [8], P('instance'), may hold values from 0 to 8191
Outputs:
- advanced: float32 [8, 3, 5, 128, 8192], P('instance', None, None, 'radial', 'sector')
The draws below stay inside these ranges and needn't reach their ends.
Inputs may be any that keep to these rules, and one draw needn't show every extreme that they name: `rotor_shift`: the rotor angle of each time instance, counted in whole cells.
All inputs are finite; a program needn't handle non-finite values.
Results may differ from the reference program's by a relative error of at most 0.00005.
Values sent between devices are 32-bit elements; how exact they have to be, the bound alone decides.
No kernel may reach another device: no remote copies, remote signals or barrier semaphores. Data moves between devices by JAX's collectives and lax.ppermute only.
A program may use at most 128 MiB of HBM per device.

```python
import jax
import jax.numpy as jnp
from jax import lax

NT = 8
VARS = 5
LAYERS = 3
GHOSTS = 2
NR = 128
NC = 8192


def with_ends(result, key, low, top_value):
    place = [jax.random.randint(jax.random.fold_in(key, axis), (), 0, length) for axis, length in enumerate(result.shape)]
    widest = result.shape.index(max(result.shape))
    next_to = place[:widest] + [(place[widest] + 1) % result.shape[widest]] + place[widest + 1:]
    return result.at[tuple(place)].set(low).at[tuple(next_to)].set(top_value)


def shard_levels(stream_key, dims, pieces, least, largest):
    def one(axis_at, parts):
        steps = jax.random.uniform(jax.random.fold_in(jax.random.fold_in(stream_key, 6), axis_at), (parts,), jnp.float32, least / len(pieces), largest / len(pieces))
        return jnp.repeat(jnp.exp(steps), dims[axis_at] // parts).reshape((-1,) + (1,) * (len(dims) - axis_at - 1))

    gain = one(*pieces[0])
    for cut in pieces[1:]:
        gain = gain * one(*cut)
    return gain


def gaussian(rng, shape, width, reach, shards=(), held_as=jnp.bfloat16):
    drawn = width * jax.random.normal(rng, shape, jnp.float32)
    if shards:
        drawn = drawn * shard_levels(rng, shape, shards, -0.22, 0.18)
    return jnp.clip(drawn, -reach, reach).astype(held_as)


def setup_inputs(seed: int = 0) -> dict:
    key_of = jax.random.split(jax.random.key(seed), 5)
    return {
        "flow_state": gaussian(key_of[0], (NT, LAYERS, VARS, NR, NC), 1.0, 6.0, ((0, 4), (3, 2), (4, 32)), jnp.float32),
        "rotor_face": gaussian(key_of[1], (NT, GHOSTS, VARS, NR, NC), 1.0, 6.0, ((0, 4), (3, 2), (4, 32)), jnp.float32),
        "jacobians": gaussian(key_of[2], (3, VARS, VARS), VARS ** -0.5, 2.5, (), jnp.float32),
        "rotor_shift": with_ends(jax.random.randint(key_of[3], (NT,), 0, NC), jax.random.fold_in(key_of[3], 1), 0, NC - 1).astype(jnp.int32),
    }


PSEUDO_STEP = 0.25
DAMPING = 0.0625
FREQUENCY = 0.5


def spectral_matrix(instance_total):
    positions = jnp.arange(instance_total, dtype=jnp.int32)
    distance = positions[:, None] - positions[None, :]
    parity_sign = (1 - 2 * (distance % 2)).astype(jnp.float32)
    angle = jnp.pi * distance.astype(jnp.float32) / instance_total
    safe_angle = jnp.where(distance == 0, jnp.float32(1.0), angle)
    values = 0.5 * parity_sign / jnp.tan(safe_angle)
    return jnp.where(distance == 0, jnp.float32(0.0), values)


def contract(matrix, field):
    return jnp.einsum("vw,lwrc->lvrc", matrix, field, precision=lax.Precision.HIGHEST)


def stencil(padded, layered, jacobians):
    radial_count = padded.shape[2] - 4
    circ_count = padded.shape[3] - 4
    layers_count = layered.shape[0] - 4

    def beside_all(offset):
        return padded[:, :, 2:2 + radial_count, 2 + offset:2 + offset + circ_count]

    def radial_at(offset):
        return padded[:, :, 2 + offset:2 + offset + radial_count, 2:2 + circ_count]

    def axial_at(offset):
        return layered[2 + offset:2 + offset + layers_count]

    def fourth(sample):
        return sample(-2) - 4.0 * sample(-1) + 6.0 * sample(0) - 4.0 * sample(1) + sample(2)

    fluxes = contract(jacobians[0], (beside_all(1) - beside_all(-1)) * 0.5)
    fluxes = fluxes + contract(jacobians[1], (radial_at(1) - radial_at(-1)) * 0.5)
    fluxes = fluxes + contract(jacobians[2], (axial_at(1) - axial_at(-1)) * 0.5)
    return fluxes + DAMPING * (fourth(beside_all) + fourth(radial_at) + fourth(axial_at))


def reference(flow_state, rotor_face, jacobians, rotor_shift):
    instance_total = flow_state.shape[0]
    shifted = jax.vmap(lambda ghosts, amount: jnp.roll(ghosts, amount, axis=-1))(rotor_face, rotor_shift)
    matrix = spectral_matrix(instance_total)
    source = jnp.dot(matrix, flow_state.reshape(instance_total, -1), precision=lax.Precision.HIGHEST)
    source = source.reshape(flow_state.shape)

    def advance(record):
        current, ghosts, spectral_part = record
        padded = jnp.pad(current, ((0, 0), (0, 0), (2, 2), (0, 0)))
        padded = jnp.pad(padded, ((0, 0), (0, 0), (0, 0), (2, 2)), mode="wrap")
        layered = jnp.concatenate([ghosts[1:2], ghosts[0:1], current, current[-1:], current[-1:]], 0)
        rates = stencil(padded, layered, jacobians)
        return current - PSEUDO_STEP * (rates + FREQUENCY * spectral_part)

    return lax.map(advance, (flow_state, shifted, source))
```

```python
import math

import jax
import jax.numpy as jnp
from jax import lax
from jax.experimental import pallas as pl
from jax.experimental.pallas import tpu as pltpu
from jax.sharding import PartitionSpec as P

PSEUDO_STEP = 0.25
DAMPING = 0.0625
FREQUENCY = 0.5

D1 = 0.5 / math.tan(math.pi / 8)
D2 = 0.5
D3 = 0.5 / math.tan(3 * math.pi / 8)

SOURCE = ((D1, 1.0, 1.0, D3, D3), (-D1, -2 * D3, -2 * D1, -2 * D3 * D3, -0.5))

SUB, LANE = 8, 128
VMEM_LIMIT = 48 * 1024 * 1024


def ring(axis, distance):
    size = lax.axis_size(axis)
    return [(i, (i + distance) % size) for i in range(size)]


def roll_kernel(shift_ref, x_ref, y_ref):
    blocks, rows, width = x_ref.shape
    whole = shift_ref[0] // width
    part = shift_ref[0] % width
    lane = lax.broadcasted_iota(jnp.int32, (rows, width), 1)
    wrapped = lane < part

    def rolled(source):
        return pltpu.roll(x_ref[source], part, 1)

    def step(d, before):
        current = rolled(lax.rem(d - whole + blocks, blocks))
        y_ref[d] = jnp.where(wrapped, before, current)
        return current

    lax.fori_loop(0, blocks, step, rolled(lax.rem(2 * blocks - 1 - whole, blocks)))


def roll_annulus(x, shift):
    return pl.pallas_call(
        roll_kernel,
        out_shape=jax.ShapeDtypeStruct(x.shape, x.dtype),
        in_specs=[
            pl.BlockSpec(memory_space=pltpu.SMEM),
            pl.BlockSpec(memory_space=pltpu.VMEM),
        ],
        out_specs=pl.BlockSpec(memory_space=pltpu.VMEM),
        compiler_params=pltpu.CompilerParams(vmem_limit_bytes=VMEM_LIMIT),
        cost_estimate=pl.CostEstimate(flops=x.size, bytes_accessed=8 * x.size, transcendentals=0),
        name="roll_annulus",
    )(shift, x)


def interior_kernel(
    jac_ref, coef_ref, u_ref, other_ref, side_ref, low_ref, high_ref,
    r1_ref, l1_ref, r2_ref, l2_ref, out_ref, first_ref, fourth_ref,
):
    layers, variables, rows, width = u_ref.shape[1:]
    n = pl.program_id(0)
    lane = lax.broadcasted_iota(jnp.int32, (rows, LANE), 1)
    sub = lax.broadcasted_iota(jnp.int32, (SUB, width), 0)
    for layer in range(layers):
        for w in range(variables):
            u = u_ref[0, layer, w]
            side = side_ref[0, layer, w]
            low8, high8 = low_ref[0, layer, w], high_ref[0, layer, w]

            def left(k):
                rim = jnp.where(lane >= LANE - k, side, u[:, width - LANE :])
                return pltpu.roll(jnp.concatenate([u[:, : width - LANE], rim], 1), k, 1)

            def right(k):
                rim = jnp.where(lane < k, side, u[:, :LANE])
                return pltpu.roll(jnp.concatenate([rim, u[:, LANE:]], 1), width - k, 1)

            def low(k):
                rim = jnp.where(sub >= SUB - k, low8, u[rows - SUB :])
                return pltpu.roll(jnp.concatenate([u[: rows - SUB], rim], 0), k, 0)

            def high(k):
                rim = jnp.where(sub < k, high8, u[:SUB])
                return pltpu.roll(jnp.concatenate([rim, u[SUB:]], 0), rows - k, 0)

            left1, right1, low1, high1 = left(1), right(1), low(1), high(1)
            near = left1 + right1 + (low1 + high1)
            far = left(2) + right(2) + (low(2) + high(2))
            next1 = u_ref[0, min(layer + 1, layers - 1), w]
            next2 = u_ref[0, min(layer + 2, layers - 1), w]
            near, far = near + next1, far + next2
            axial = next1
            if layer >= 1:
                previous = u_ref[0, layer - 1, w]
                near, axial = near + previous, axial - previous
            if layer >= 2:
                far = far + u_ref[0, layer - 2, w]
            first_ref[w] = right1 - left1
            first_ref[variables + w] = high1 - low1
            first_ref[2 * variables + w] = axial
            fourth_ref[w] = far - 4.0 * near + 18.0 * u

        def tile(t, carry):
            at = pl.ds(pl.multiple_of(t * SUB, SUB), SUB)
            firsts = [first_ref[k, at] for k in range(3 * variables)]
            for v in range(variables):
                value = u_ref[0, layer, v, at] - (PSEUDO_STEP * DAMPING) * fourth_ref[v, at]
                source = coef_ref[n, 0] * other_ref[0, layer, v, at]
                for k, ref in enumerate((r1_ref, l1_ref, r2_ref, l2_ref)):
                    source = source + coef_ref[n, k + 1] * ref[layer, v, at]
                value = value - source
                for d in range(3):
                    for w in range(variables):
                        k = (d * variables + v) * variables + w
                        value = value - jac_ref[k] * firsts[d * variables + w]
                out_ref[0, layer, v, at] = value
            return carry

        lax.fori_loop(0, rows // SUB, tile, 0)


def interior(flow, side, low, high, received, jac, coef):
    instances, layers, variables, rows, width = flow.shape
    smem = pl.BlockSpec(memory_space=pltpu.SMEM)

    def own(shape):
        return pl.BlockSpec((1,) + shape[1:], lambda n: (n, 0, 0, 0, 0))

    other = pl.BlockSpec((1,) + flow.shape[1:], lambda n: (1 - n, 0, 0, 0, 0))
    field = pl.BlockSpec(flow.shape[1:], lambda n: (0, 0, 0, 0))
    return pl.pallas_call(
        interior_kernel,
        grid=(instances,),
        out_shape=jax.ShapeDtypeStruct(flow.shape, flow.dtype),
        in_specs=[smem, smem, own(flow.shape), other, own(side.shape), own(low.shape), own(high.shape)]
        + [field] * 4,
        out_specs=own(flow.shape),
        scratch_shapes=[
            pltpu.VMEM((3 * variables, rows, width), jnp.float32),
            pltpu.VMEM((variables, rows, width), jnp.float32),
        ],
        compiler_params=pltpu.CompilerParams(vmem_limit_bytes=VMEM_LIMIT),
        cost_estimate=pl.CostEstimate(
            flops=80 * flow.size, bytes_accessed=20 * flow.size, transcendentals=0
        ),
        name="interior",
    )(jac, coef, flow, flow, side, low, high, *received)


def ghosts_kernel(jac_ref, part_ref, ghost_ref, out_ref):
    variables, rows = part_ref.shape[2], part_ref.shape[3]

    def tile(t, carry):
        at = pl.ds(pl.multiple_of(t * SUB, SUB), SUB)
        nearest = [ghost_ref[0, 0, w, at] for w in range(variables)]
        for v in range(variables):
            value = part_ref[0, 0, v, at]
            value = value - (PSEUDO_STEP * DAMPING) * (ghost_ref[0, 1, v, at] - 4.0 * nearest[v])
            for w in range(variables):
                value = value + jac_ref[(2 * variables + v) * variables + w] * nearest[w]
            out_ref[0, 0, v, at] = value
            out_ref[0, 1, v, at] = part_ref[0, 1, v, at] - (PSEUDO_STEP * DAMPING) * nearest[v]
        return carry

    lax.fori_loop(0, rows // SUB, tile, 0)


def add_ghosts(part, ghosts, jac):
    instances, _, variables, rows, width = part.shape
    block = (1, 2, variables, rows, width)
    spec = pl.BlockSpec(block, lambda n: (n, 0, 0, 0, 0))
    return pl.pallas_call(
        ghosts_kernel,
        grid=(instances,),
        out_shape=jax.ShapeDtypeStruct(part.shape, part.dtype),
        in_specs=[pl.BlockSpec(memory_space=pltpu.SMEM), spec, spec],
        out_specs=spec,
        input_output_aliases={1: 0},
        compiler_params=pltpu.CompilerParams(vmem_limit_bytes=VMEM_LIMIT),
        cost_estimate=pl.CostEstimate(
            flops=20 * ghosts.size, bytes_accessed=12 * ghosts.size, transcendentals=0
        ),
        name="add_ghosts",
    )(jac, part, ghosts)


def on_device(flow, rotor, jacobians, rotor_shift):
    sectors = lax.axis_size("sector")
    sector = lax.axis_index("sector")
    radial = lax.axis_index("radial")
    instances, layers, variables, rows, width = flow.shape

    pieces = rotor.reshape(sectors, -1, width)
    held = lax.all_to_all(pieces, "sector", 0, 0)

    to_right = D2 * flow[0] - D1 * flow[1]
    to_left = D3 * flow[1] - D2 * flow[0]
    r1 = lax.ppermute(to_right, "instance", ring("instance", 1))
    l1 = lax.ppermute(to_left, "instance", ring("instance", -1))
    held, r1, l1 = lax.optimization_barrier((held, r1, l1))
    r2 = lax.ppermute(r1, "instance", ring("instance", 1))
    l2 = lax.ppermute(l1, "instance", ring("instance", -1))

    shift = lax.dynamic_slice_in_dim(rotor_shift, sector * instances // sectors, 1)
    rolled = roll_annulus(held, shift)
    ghosts = lax.all_to_all(rolled, "sector", 0, 0).reshape(rotor.shape)

    before = lax.ppermute(flow[..., width - 2 :].swapaxes(3, 4), "sector", ring("sector", 1)).swapaxes(3, 4)
    after = lax.ppermute(flow[..., :2].swapaxes(3, 4), "sector", ring("sector", -1)).swapaxes(3, 4)
    side = jnp.concatenate(
        [after, jnp.zeros(flow.shape[:-1] + (LANE - 4,), flow.dtype), before], -1
    )
    rim = jnp.where(radial == 0, flow[:, :, :, rows - 2 :], flow[:, :, :, :2])
    rim = lax.ppermute(rim, "radial", ring("radial", 1))
    low = jnp.pad(jnp.where(radial == 0, 0.0, rim), ((0, 0),) * 3 + ((SUB - 2, 0), (0, 0)))
    high = jnp.pad(jnp.where(radial == 0, rim, 0.0), ((0, 0),) * 3 + ((0, SUB - 2), (0, 0)))

    jac = jacobians.reshape(-1) * (0.5 * PSEUDO_STEP)
    coef = jnp.asarray(SOURCE, jnp.float32) * (PSEUDO_STEP * FREQUENCY)
    part = interior(flow, side, low, high, (r1, l1, r2, l2), jac, coef)
    return add_ghosts(part, ghosts, jac)


def solution(mesh):
    return jax.shard_map(
        on_device,
        mesh=mesh,
        in_specs=(
            P("instance", None, None, "radial", "sector"),
            P("instance", None, None, "radial", "sector"),
            P(),
            P("instance"),
        ),
        out_specs=P("instance", None, None, "radial", "sector"),
        check_vma=False,
    )
```

```python
import math

import jax
import jax.numpy as jnp
from jax import lax
from jax.experimental import pallas as pl
from jax.experimental.pallas import tpu as pltpu
from jax.sharding import PartitionSpec as P

PSEUDO_STEP = 0.25
DAMPING = 0.0625
FREQUENCY = 0.5

D1 = 0.5 / math.tan(math.pi / 8)
D2 = 0.5
D3 = 0.5 / math.tan(3 * math.pi / 8)

SOURCE = ((D1, 1.0, 1.0, D3, D3), (-D1, -2 * D3, -2 * D1, -2 * D3 * D3, -0.5))

SUB, LANE = 8, 128
MIB = 1024 * 1024


def ring(axis, distance):
    size = lax.axis_size(axis)
    return [(i, (i + distance) % size) for i in range(size)]


def turn_kernel(shift_ref, x_ref, y_ref):
    blocks, rows, width = x_ref.shape
    halves = width // LANE
    strips = blocks * halves
    whole = shift_ref[0] // LANE
    kept = lax.broadcasted_iota(jnp.int32, (rows, LANE), 1) < LANE - shift_ref[0] % LANE

    def strip(index):
        at = pl.multiple_of(lax.rem(index, halves) * LANE, LANE)
        return x_ref[index // halves, :, pl.ds(at, LANE)]

    def step(d, before):
        for h in range(halves):
            current = strip(lax.rem(d * halves + h - whole + strips, strips))
            y_ref[d, :, h * LANE : (h + 1) * LANE] = jnp.where(kept, current, before)
            before = current
        return before

    lax.fori_loop(0, blocks, step, strip(lax.rem(2 * strips - 1 - whole, strips)), unroll=8)


def turn_annulus(x, shift):
    return pl.pallas_call(
        turn_kernel,
        out_shape=jax.ShapeDtypeStruct(x.shape, x.dtype),
        in_specs=[
            pl.BlockSpec(memory_space=pltpu.SMEM),
            pl.BlockSpec(memory_space=pltpu.VMEM),
        ],
        out_specs=pl.BlockSpec(memory_space=pltpu.VMEM),
        compiler_params=pltpu.CompilerParams(vmem_limit_bytes=8 * MIB),
        cost_estimate=pl.CostEstimate(flops=x.size, bytes_accessed=8 * x.size, transcendentals=0),
        name="turn_annulus",
    )(shift, x)


def interior_kernel(
    jac_ref, u_ref, side_ref, low_ref, high_ref,
    r1_ref, l1_ref, out_ref, first_ref, fourth_ref,
):
    instances, layers, variables, rows, width = u_ref.shape
    lane = lax.broadcasted_iota(jnp.int32, (rows, LANE), 1)
    sub = lax.broadcasted_iota(jnp.int32, (SUB, width), 0)
    for n in range(instances):
        for layer in range(layers):
            for w in range(variables):
                u = u_ref[n, layer, w]
                side = side_ref[n, layer, w]
                low8, high8 = low_ref[n, layer, w], high_ref[n, layer, w]

                def left(k):
                    rim = jnp.where(lane >= LANE - k, side, u[:, width - LANE :])
                    return pltpu.roll(jnp.concatenate([u[:, : width - LANE], rim], 1), k, 1)

                def right(k):
                    rim = jnp.where(lane < k, side, u[:, :LANE])
                    return pltpu.roll(jnp.concatenate([rim, u[:, LANE:]], 1), width - k, 1)

                def low(k):
                    rim = jnp.where(sub >= SUB - k, low8, u[rows - SUB :])
                    return pltpu.roll(jnp.concatenate([u[: rows - SUB], rim], 0), k, 0)

                def high(k):
                    rim = jnp.where(sub < k, high8, u[:SUB])
                    return pltpu.roll(jnp.concatenate([rim, u[SUB:]], 0), rows - k, 0)

                left1, right1, low1, high1 = left(1), right(1), low(1), high(1)
                near = left1 + right1 + (low1 + high1)
                far = left(2) + right(2) + (low(2) + high(2))
                next1 = u_ref[n, min(layer + 1, layers - 1), w]
                next2 = u_ref[n, min(layer + 2, layers - 1), w]
                near, far = near + next1, far + next2
                axial = next1
                if layer >= 1:
                    previous = u_ref[n, layer - 1, w]
                    near, axial = near + previous, axial - previous
                if layer >= 2:
                    far = far + u_ref[n, layer - 2, w]
                first_ref[w] = right1 - left1
                first_ref[variables + w] = high1 - low1
                first_ref[2 * variables + w] = axial
                fourth_ref[w] = far - 4.0 * near + 18.0 * u

            def tile(t, carry):
                at = pl.ds(pl.multiple_of(t * SUB, SUB), SUB)
                firsts = [first_ref[k, at] for k in range(3 * variables)]
                for v in range(variables):
                    value = u_ref[n, layer, v, at] - (PSEUDO_STEP * DAMPING) * fourth_ref[v, at]
                    source = SOURCE[n][0] * u_ref[1 - n, layer, v, at]
                    for k, ref in enumerate((r1_ref, l1_ref)):
                        source = source + SOURCE[n][k + 1] * ref[layer, v, at]
                    value = value - (PSEUDO_STEP * FREQUENCY) * source
                    for d in range(3):
                        for w in range(variables):
                            k = (d * variables + v) * variables + w
                            value = value - jac_ref[k] * firsts[d * variables + w]
                    out_ref[n, layer, v, at] = value
                return carry

            lax.fori_loop(0, rows // SUB, tile, 0)


def interior(flow, side, low, high, received, jac):
    variables, rows, width = flow.shape[2:]
    whole = pl.BlockSpec(memory_space=pltpu.VMEM)
    return pl.pallas_call(
        interior_kernel,
        out_shape=jax.ShapeDtypeStruct(flow.shape, flow.dtype),
        in_specs=[pl.BlockSpec(memory_space=pltpu.SMEM)] + [whole] * 6,
        out_specs=whole,
        scratch_shapes=[
            pltpu.VMEM((3 * variables, rows, width), jnp.float32),
            pltpu.VMEM((variables, rows, width), jnp.float32),
        ],
        compiler_params=pltpu.CompilerParams(vmem_limit_bytes=24 * MIB),
        cost_estimate=pl.CostEstimate(
            flops=80 * flow.size, bytes_accessed=20 * flow.size, transcendentals=0
        ),
        name="interior",
    )(jac, flow, side, low, high, *received)


def ghosts_kernel(shift_ref, jac_ref, part_ref, ghost_ref, out_ref):
    variables, rows, width = part_ref.shape[2:]
    amount = shift_ref[pl.program_id(0)] % LANE
    for at in range(0, width, LANE):
        lanes = slice(at, at + LANE)
        nearest = [pltpu.roll(ghost_ref[0, 0, w, :, lanes], amount, 1) for w in range(variables)]
        for v in range(variables):
            value = part_ref[0, 0, v, :, lanes] + (4.0 * PSEUDO_STEP * DAMPING) * nearest[v]
            second = pltpu.roll(ghost_ref[0, 1, v, :, lanes], amount, 1)
            value = value - (PSEUDO_STEP * DAMPING) * second
            for w in range(variables):
                value = value + jac_ref[(2 * variables + v) * variables + w] * nearest[w]
            out_ref[0, 0, v, :, lanes] = value
            out_ref[0, 1, v, :, lanes] = part_ref[0, 1, v, :, lanes] - (PSEUDO_STEP * DAMPING) * nearest[v]


def add_ghosts(part, ghosts, shift, jac):
    instances, _, variables, rows, width = part.shape
    chunk = 4 * SUB
    spec = pl.BlockSpec((1, 2, variables, chunk, width), lambda n, t: (n, 0, 0, t, 0))
    smem = pl.BlockSpec(memory_space=pltpu.SMEM)
    return pl.pallas_call(
        ghosts_kernel,
        grid=(instances, rows // chunk),
        out_shape=jax.ShapeDtypeStruct(part.shape, part.dtype),
        in_specs=[smem, smem, spec, spec],
        out_specs=spec,
        input_output_aliases={2: 0},
        compiler_params=pltpu.CompilerParams(vmem_limit_bytes=8 * MIB),
        cost_estimate=pl.CostEstimate(
            flops=20 * ghosts.size, bytes_accessed=12 * ghosts.size, transcendentals=0
        ),
        name="add_ghosts",
    )(shift, jac, part, ghosts)


def on_device(flow, rotor, jacobians, rotor_shift):
    sectors = lax.axis_size("sector")
    sector = lax.axis_index("sector")
    radial = lax.axis_index("radial")
    instances, layers, variables, rows, width = flow.shape

    held = lax.all_to_all(rotor.reshape(sectors, -1, width), "sector", 0, 0)

    to_right = D2 * flow[0] - D1 * flow[1]
    to_left = D3 * flow[1] - D2 * flow[0]
    r1 = lax.ppermute(to_right, "instance", ring("instance", 1))
    l1 = lax.ppermute(to_left, "instance", ring("instance", -1))

    before = lax.ppermute(flow[..., width - 2 :].swapaxes(3, 4), "sector", ring("sector", 1))
    after = lax.ppermute(flow[..., :2].swapaxes(3, 4), "sector", ring("sector", -1))
    rim = jnp.where(radial == 0, flow[:, :, :, rows - 2 :], flow[:, :, :, :2])
    rim = lax.ppermute(rim, "radial", ring("radial", 1))

    held, r1, l1, before, after, rim = lax.optimization_barrier((held, r1, l1, before, after, rim))
    r2 = lax.ppermute(r1, "instance", ring("instance", 1))
    l2 = lax.ppermute(l1, "instance", ring("instance", -1))
    own_shift = lax.dynamic_slice_in_dim(rotor_shift, sector * instances // sectors, 1)
    ghosts = lax.all_to_all(turn_annulus(held, own_shift), "sector", 0, 0).reshape(rotor.shape)

    middle = jnp.zeros(flow.shape[:-1] + (LANE - 4,), flow.dtype)
    side = jnp.concatenate([after.swapaxes(3, 4), middle, before.swapaxes(3, 4)], -1)
    low = jnp.pad(jnp.where(radial == 0, 0.0, rim), ((0, 0),) * 3 + ((SUB - 2, 0), (0, 0)))
    high = jnp.pad(jnp.where(radial == 0, rim, 0.0), ((0, 0),) * 3 + ((0, SUB - 2), (0, 0)))
    jac = jacobians.reshape(-1) * (0.5 * PSEUDO_STEP)
    part = interior(flow, side, low, high, (r1, l1), jac)
    far = jnp.stack([row[3] * r2 + row[4] * l2 for row in SOURCE])
    part = part - (PSEUDO_STEP * FREQUENCY) * far
    return add_ghosts(part, ghosts, rotor_shift, jac)


def solution(mesh):
    return jax.shard_map(
        on_device,
        mesh=mesh,
        in_specs=(
            P("instance", None, None, "radial", "sector"),
            P("instance", None, None, "radial", "sector"),
            P(),
            P("instance"),
        ),
        out_specs=P("instance", None, None, "radial", "sector"),
        check_vma=False,
    )
```

```python
import functools
import math

import jax
import jax.numpy as jnp
from jax import lax
from jax.experimental import pallas as pl
from jax.experimental.pallas import tpu as pltpu
from jax.sharding import PartitionSpec as P

PSEUDO_STEP = 0.25
DAMPING = 0.0625
FREQUENCY = 0.5

D1 = 0.5 / math.tan(math.pi / 8)
D2 = 0.5
D3 = 0.5 / math.tan(3 * math.pi / 8)

SOURCE = ((D1, 1.0, 1.0, D3, D3), (-D1, -2 * D3, -2 * D1, -2 * D3 * D3, -0.5))

SUB, LANE = 8, 128
MIB = 1024 * 1024


def ring(axis, distance):
    size = lax.axis_size(axis)
    return [(i, (i + distance) % size) for i in range(size)]


def turn_kernel(parts, shift_ref, x_ref, y_ref, held_ref, sems):
    blocks, rows, width = x_ref.shape
    halves = width // LANE
    strips = blocks * halves
    whole = shift_ref[0] // LANE
    kept = lax.broadcasted_iota(jnp.int32, (rows, LANE), 1) < LANE - shift_ref[0] % LANE

    def strip(index):
        at = pl.multiple_of(lax.rem(index, halves) * LANE, LANE)
        return x_ref[index // halves, :, pl.ds(at, LANE)]

    def step(d, before):
        for h in range(halves):
            current = strip(lax.rem(d * halves + h - whole + strips, strips))
            held_ref[d, :, h * LANE : (h + 1) * LANE] = jnp.where(kept, current, before)
            before = current
        return before

    before = strip(lax.rem(2 * strips - 1 - whole, strips))
    copies = []
    for part in range(parts):
        first, count = part * (blocks // parts), blocks // parts
        before = lax.fori_loop(first, first + count, step, before, unroll=8)
        at = pl.ds(first, count)
        copies.append(pltpu.make_async_copy(held_ref.at[at], y_ref.at[at], sems.at[part]))
        copies[-1].start()
    for copy in copies:
        copy.wait()


def turn_annulus(x, shift):
    parts = 4
    return pl.pallas_call(
        functools.partial(turn_kernel, parts),
        out_shape=pltpu.HBM(x.shape, x.dtype),
        in_specs=[
            pl.BlockSpec(memory_space=pltpu.SMEM),
            pl.BlockSpec(memory_space=pltpu.VMEM),
        ],
        out_specs=pl.BlockSpec(memory_space=pltpu.HBM),
        scratch_shapes=[pltpu.VMEM(x.shape, x.dtype), pltpu.SemaphoreType.DMA((parts,))],
        compiler_params=pltpu.CompilerParams(vmem_limit_bytes=8 * MIB),
        cost_estimate=pl.CostEstimate(flops=x.size, bytes_accessed=8 * x.size, transcendentals=0),
        name="turn_annulus",
    )(shift, x)


def interior_kernel(
    jac_ref, u_ref, side_ref, low_ref, high_ref,
    r1_ref, l1_ref, out_ref, first_ref, fourth_ref,
):
    instances, layers, variables, rows, width = u_ref.shape
    lane = lax.broadcasted_iota(jnp.int32, (rows, LANE), 1)
    sub = lax.broadcasted_iota(jnp.int32, (SUB, width), 0)
    for n in range(instances):
        for layer in range(layers):
            for w in range(variables):
                u = u_ref[n, layer, w]
                side = side_ref[n, layer, w]
                low8, high8 = low_ref[n, layer, w], high_ref[n, layer, w]

                def left(k):
                    rim = jnp.where(lane >= LANE - k, side, u[:, width - LANE :])
                    return pltpu.roll(jnp.concatenate([u[:, : width - LANE], rim], 1), k, 1)

                def right(k):
                    rim = jnp.where(lane < k, side, u[:, :LANE])
                    return pltpu.roll(jnp.concatenate([rim, u[:, LANE:]], 1), width - k, 1)

                def low(k):
                    rim = jnp.where(sub >= SUB - k, low8, u[rows - SUB :])
                    return pltpu.roll(jnp.concatenate([u[: rows - SUB], rim], 0), k, 0)

                def high(k):
                    rim = jnp.where(sub < k, high8, u[:SUB])
                    return pltpu.roll(jnp.concatenate([rim, u[SUB:]], 0), rows - k, 0)

                left1, right1, low1, high1 = left(1), right(1), low(1), high(1)
                near = left1 + right1 + (low1 + high1)
                far = left(2) + right(2) + (low(2) + high(2))
                next1 = u_ref[n, min(layer + 1, layers - 1), w]
                next2 = u_ref[n, min(layer + 2, layers - 1), w]
                near, far = near + next1, far + next2
                axial = next1
                if layer >= 1:
                    previous = u_ref[n, layer - 1, w]
                    near, axial = near + previous, axial - previous
                if layer >= 2:
                    far = far + u_ref[n, layer - 2, w]
                first_ref[w] = right1 - left1
                first_ref[variables + w] = high1 - low1
                first_ref[2 * variables + w] = axial
                fourth_ref[w] = far - 4.0 * near + 18.0 * u

            def tile(t, carry):
                at = pl.ds(pl.multiple_of(t * SUB, SUB), SUB)
                firsts = [first_ref[k, at] for k in range(3 * variables)]
                for v in range(variables):
                    value = u_ref[n, layer, v, at] - (PSEUDO_STEP * DAMPING) * fourth_ref[v, at]
                    source = SOURCE[n][0] * u_ref[1 - n, layer, v, at]
                    for k, ref in enumerate((r1_ref, l1_ref)):
                        source = source + SOURCE[n][k + 1] * ref[layer, v, at]
                    value = value - (PSEUDO_STEP * FREQUENCY) * source
                    for d in range(3):
                        for w in range(variables):
                            k = (d * variables + v) * variables + w
                            value = value - jac_ref[k] * firsts[d * variables + w]
                    out_ref[n, layer, v, at] = value
                return carry

            lax.fori_loop(0, rows // SUB, tile, 0)


def interior(flow, side, low, high, received, jac):
    variables, rows, width = flow.shape[2:]
    whole = pl.BlockSpec(memory_space=pltpu.VMEM)
    return pl.pallas_call(
        interior_kernel,
        out_shape=jax.ShapeDtypeStruct(flow.shape, flow.dtype),
        in_specs=[pl.BlockSpec(memory_space=pltpu.SMEM)] + [whole] * 6,
        out_specs=whole,
        scratch_shapes=[
            pltpu.VMEM((3 * variables, rows, width), jnp.float32),
            pltpu.VMEM((variables, rows, width), jnp.float32),
        ],
        compiler_params=pltpu.CompilerParams(vmem_limit_bytes=24 * MIB),
        cost_estimate=pl.CostEstimate(
            flops=80 * flow.size, bytes_accessed=20 * flow.size, transcendentals=0
        ),
        name="interior",
    )(jac, flow, side, low, high, *received)


def ghosts_kernel(parts, shift_ref, jac_ref, part_ref, ghost_ref, out_ref, held_ref, last_sems, sems):
    instances, layers, variables, rows, width = part_ref.shape
    copies = []
    for n in range(instances):
        for layer in range(2, layers):
            copies.append(
                pltpu.make_async_copy(part_ref.at[n, layer], out_ref.at[n, layer], last_sems.at[n, layer - 2])
            )
            copies[-1].start()

    def tile(n, t):
        amount = shift_ref[n] % LANE
        at = pl.ds(pl.multiple_of(t * SUB, SUB), SUB)
        for first in range(0, width, LANE):
            lanes = slice(first, first + LANE)
            nearest = [pltpu.roll(ghost_ref[n, 0, w, at, lanes], amount, 1) for w in range(variables)]
            for v in range(variables):
                value = part_ref[n, 0, v, at, lanes] + (4.0 * PSEUDO_STEP * DAMPING) * nearest[v]
                second = pltpu.roll(ghost_ref[n, 1, v, at, lanes], amount, 1)
                value = value - (PSEUDO_STEP * DAMPING) * second
                for w in range(variables):
                    value = value + jac_ref[(2 * variables + v) * variables + w] * nearest[w]
                held_ref[n, 0, v, at, lanes] = value
                held_ref[n, 1, v, at, lanes] = part_ref[n, 1, v, at, lanes] - (PSEUDO_STEP * DAMPING) * nearest[v]

    count = rows // parts
    for n in range(instances):
        for part in range(parts):
            for t in range(part * count // SUB, (part + 1) * count // SUB):
                tile(n, t)
            at = pl.ds(part * count, count)
            copies.append(
                pltpu.make_async_copy(
                    held_ref.at[n, :, :, at], out_ref.at[n, pl.ds(0, 2), :, at], sems.at[n, part]
                )
            )
            copies[-1].start()
    for copy in copies:
        copy.wait()


def add_ghosts(part, ghosts, shift, jac):
    instances, layers = part.shape[:2]
    parts = 2
    smem, vmem = (pl.BlockSpec(memory_space=space) for space in (pltpu.SMEM, pltpu.VMEM))
    return pl.pallas_call(
        functools.partial(ghosts_kernel, parts),
        out_shape=jax.ShapeDtypeStruct(part.shape, part.dtype),
        in_specs=[smem, smem, vmem, vmem],
        out_specs=pl.BlockSpec(memory_space=pltpu.HBM),
        scratch_shapes=[
            pltpu.VMEM((instances, 2) + part.shape[2:], part.dtype),
            pltpu.SemaphoreType.DMA((instances, layers - 2)),
            pltpu.SemaphoreType.DMA((instances, parts)),
        ],
        compiler_params=pltpu.CompilerParams(vmem_limit_bytes=12 * MIB),
        cost_estimate=pl.CostEstimate(
            flops=20 * ghosts.size, bytes_accessed=12 * ghosts.size, transcendentals=0
        ),
        name="add_ghosts",
    )(shift, jac, part, pltpu.with_memory_space_constraint(ghosts, pltpu.VMEM))


def on_device(flow, rotor, jacobians, rotor_shift):
    sectors = lax.axis_size("sector")
    sector = lax.axis_index("sector")
    radial = lax.axis_index("radial")
    instances, layers, variables, rows, width = flow.shape

    held = lax.all_to_all(rotor.reshape(sectors, -1, width), "sector", 0, 0)

    to_right = D2 * flow[0] - D1 * flow[1]
    to_left = D3 * flow[1] - D2 * flow[0]
    r1 = lax.ppermute(to_right, "instance", ring("instance", 1))
    l1 = lax.ppermute(to_left, "instance", ring("instance", -1))

    before = lax.ppermute(flow[..., width - 2 :].swapaxes(3, 4), "sector", ring("sector", 1))
    after = lax.ppermute(flow[..., :2].swapaxes(3, 4), "sector", ring("sector", -1))
    rim = jnp.where(radial == 0, flow[:, :, :, rows - 2 :], flow[:, :, :, :2])
    rim = lax.ppermute(rim, "radial", ring("radial", 1))

    held, r1, l1, before, after, rim = lax.optimization_barrier((held, r1, l1, before, after, rim))
    r2 = lax.ppermute(r1, "instance", ring("instance", 1))
    l2 = lax.ppermute(l1, "instance", ring("instance", -1))
    own_shift = lax.dynamic_slice_in_dim(rotor_shift, sector * instances // sectors, 1)
    ghosts = lax.all_to_all(turn_annulus(held, own_shift), "sector", 0, 0).reshape(rotor.shape)

    middle = jnp.zeros(flow.shape[:-1] + (LANE - 4,), flow.dtype)
    side = jnp.concatenate([after.swapaxes(3, 4), middle, before.swapaxes(3, 4)], -1)
    low = jnp.pad(jnp.where(radial == 0, 0.0, rim), ((0, 0),) * 3 + ((SUB - 2, 0), (0, 0)))
    high = jnp.pad(jnp.where(radial == 0, rim, 0.0), ((0, 0),) * 3 + ((0, SUB - 2), (0, 0)))
    jac = jacobians.reshape(-1) * (0.5 * PSEUDO_STEP)
    part = interior(flow, side, low, high, (r1, l1), jac)
    far = jnp.stack([row[3] * r2 + row[4] * l2 for row in SOURCE])
    part = part - (PSEUDO_STEP * FREQUENCY) * far
    return add_ghosts(part, ghosts, rotor_shift, jac)


def solution(mesh):
    return jax.shard_map(
        on_device,
        mesh=mesh,
        in_specs=(
            P("instance", None, None, "radial", "sector"),
            P("instance", None, None, "radial", "sector"),
            P(),
            P("instance"),
        ),
        out_specs=P("instance", None, None, "radial", "sector"),
        check_vma=False,
    )
```

```python
import functools
import math

import jax
import jax.numpy as jnp
from jax import lax
from jax.experimental import pallas as pl
from jax.experimental.pallas import tpu as pltpu
from jax.sharding import PartitionSpec as P

PSEUDO_STEP = 0.25
DAMPING = 0.0625
FREQUENCY = 0.5

D1 = 0.5 / math.tan(math.pi / 8)
D2 = 0.5
D3 = 0.5 / math.tan(3 * math.pi / 8)

SOURCE = ((D1, 1.0, 1.0, D3, D3), (-D1, -2 * D3, -2 * D1, -2 * D3 * D3, -0.5))

ORDER = (
    20, 7, 5, 2, 3, 21, 13, 28, 12, 1, 19, 14, 18, 6, 11, 23,
    24, 30, 22, 10, 27, 31, 8, 26, 16, 25, 17, 0, 15, 4, 29, 9,
)

SUB, LANE = 8, 128
MIB = 1024 * 1024


def ring(axis, distance):
    size = lax.axis_size(axis)
    return [(i, (i + distance) % size) for i in range(size)]


def turn_kernel(parts, table_ref, x_ref, y_ref, held_ref, sems):
    blocks, rows, width = x_ref.shape
    halves = width // LANE
    strips = blocks * halves
    whole = table_ref[0] // LANE
    kept = lax.broadcasted_iota(jnp.int32, (rows, LANE), 1) < LANE - table_ref[0] % LANE

    def strip(index):
        index = lax.rem(index - whole + 2 * strips, strips)
        at = pl.multiple_of(lax.rem(index, halves) * LANE, LANE)
        return x_ref[table_ref[1 + blocks + index // halves], :, pl.ds(at, LANE)]

    def step(slot, carry):
        first = table_ref[1 + slot] * halves
        before = strip(first - 1)
        for h in range(halves):
            current = strip(first + h)
            held_ref[slot, :, h * LANE : (h + 1) * LANE] = jnp.where(kept, current, before)
            before = current
        return carry

    copies = []
    for part in range(parts):
        first, count = part * (blocks // parts), blocks // parts
        lax.fori_loop(first, first + count, step, 0, unroll=8)
        at = pl.ds(first, count)
        copies.append(pltpu.make_async_copy(held_ref.at[at], y_ref.at[at], sems.at[part]))
        copies[-1].start()
    for copy in copies:
        copy.wait()


def turn_annulus(x, table):
    parts = 4
    return pl.pallas_call(
        functools.partial(turn_kernel, parts),
        out_shape=pltpu.HBM(x.shape, x.dtype),
        in_specs=[
            pl.BlockSpec(memory_space=pltpu.SMEM),
            pl.BlockSpec(memory_space=pltpu.VMEM),
        ],
        out_specs=pl.BlockSpec(memory_space=pltpu.HBM),
        scratch_shapes=[pltpu.VMEM(x.shape, x.dtype), pltpu.SemaphoreType.DMA((parts,))],
        compiler_params=pltpu.CompilerParams(vmem_limit_bytes=8 * MIB),
        cost_estimate=pl.CostEstimate(flops=x.size, bytes_accessed=8 * x.size, transcendentals=0),
        name="turn_annulus",
    )(table, x)


def interior_kernel(
    jac_ref, u_ref, side_ref, low_ref, high_ref,
    r1_ref, l1_ref, out_ref, first_ref, fourth_ref,
):
    instances, layers, variables, rows, width = u_ref.shape
    lane = lax.broadcasted_iota(jnp.int32, (rows, LANE), 1)
    sub = lax.broadcasted_iota(jnp.int32, (SUB, width), 0)
    for n in range(instances):
        for layer in range(layers):
            for w in range(variables):
                u = u_ref[n, layer, w]
                side = side_ref[n, layer, w]
                low8, high8 = low_ref[n, layer, w], high_ref[n, layer, w]

                def left(k):
                    rim = jnp.where(lane >= LANE - k, side, u[:, width - LANE :])
                    return pltpu.roll(jnp.concatenate([u[:, : width - LANE], rim], 1), k, 1)

                def right(k):
                    rim = jnp.where(lane < k, side, u[:, :LANE])
                    return pltpu.roll(jnp.concatenate([rim, u[:, LANE:]], 1), width - k, 1)

                def low(k):
                    rim = jnp.where(sub >= SUB - k, low8, u[rows - SUB :])
                    return pltpu.roll(jnp.concatenate([u[: rows - SUB], rim], 0), k, 0)

                def high(k):
                    rim = jnp.where(sub < k, high8, u[:SUB])
                    return pltpu.roll(jnp.concatenate([rim, u[SUB:]], 0), rows - k, 0)

                left1, right1, low1, high1 = left(1), right(1), low(1), high(1)
                near = left1 + right1 + (low1 + high1)
                far = left(2) + right(2) + (low(2) + high(2))
                next1 = u_ref[n, min(layer + 1, layers - 1), w]
                next2 = u_ref[n, min(layer + 2, layers - 1), w]
                near, far = near + next1, far + next2
                axial = next1
                if layer >= 1:
                    previous = u_ref[n, layer - 1, w]
                    near, axial = near + previous, axial - previous
                if layer >= 2:
                    far = far + u_ref[n, layer - 2, w]
                first_ref[w] = right1 - left1
                first_ref[variables + w] = high1 - low1
                first_ref[2 * variables + w] = axial
                fourth_ref[w] = far - 4.0 * near + 18.0 * u

            def tile(t, carry):
                at = pl.ds(pl.multiple_of(t * SUB, SUB), SUB)
                firsts = [first_ref[k, at] for k in range(3 * variables)]
                for v in range(variables):
                    value = u_ref[n, layer, v, at] - (PSEUDO_STEP * DAMPING) * fourth_ref[v, at]
                    source = SOURCE[n][0] * u_ref[1 - n, layer, v, at]
                    for k, ref in enumerate((r1_ref, l1_ref)):
                        source = source + SOURCE[n][k + 1] * ref[layer, v, at]
                    value = value - (PSEUDO_STEP * FREQUENCY) * source
                    for d in range(3):
                        for w in range(variables):
                            k = (d * variables + v) * variables + w
                            value = value - jac_ref[k] * firsts[d * variables + w]
                    out_ref[n, layer, v, at] = value
                return carry

            lax.fori_loop(0, rows // SUB, tile, 0)


def interior(flow, side, low, high, received, jac):
    variables, rows, width = flow.shape[2:]
    whole = pl.BlockSpec(memory_space=pltpu.VMEM)
    return pl.pallas_call(
        interior_kernel,
        out_shape=jax.ShapeDtypeStruct(flow.shape, flow.dtype),
        in_specs=[pl.BlockSpec(memory_space=pltpu.SMEM)] + [whole] * 6,
        out_specs=whole,
        scratch_shapes=[
            pltpu.VMEM((3 * variables, rows, width), jnp.float32),
            pltpu.VMEM((variables, rows, width), jnp.float32),
        ],
        compiler_params=pltpu.CompilerParams(vmem_limit_bytes=24 * MIB),
        cost_estimate=pl.CostEstimate(
            flops=80 * flow.size, bytes_accessed=20 * flow.size, transcendentals=0
        ),
        name="interior",
    )(jac, flow, side, low, high, *received)


def ghosts_kernel(parts, shift_ref, jac_ref, part_ref, ghost_ref, out_ref, held_ref, last_sems, sems):
    instances, layers, variables, rows, width = part_ref.shape
    copies = []
    for n in range(instances):
        for layer in range(2, layers):
            copies.append(
                pltpu.make_async_copy(part_ref.at[n, layer], out_ref.at[n, layer], last_sems.at[n, layer - 2])
            )
            copies[-1].start()

    def tile(n, t):
        amount = shift_ref[n] % LANE
        at = pl.ds(pl.multiple_of(t * SUB, SUB), SUB)
        for first in range(0, width, LANE):
            lanes = slice(first, first + LANE)
            nearest = [pltpu.roll(ghost_ref[n, 0, w, at, lanes], amount, 1) for w in range(variables)]
            for v in range(variables):
                value = part_ref[n, 0, v, at, lanes] + (4.0 * PSEUDO_STEP * DAMPING) * nearest[v]
                second = pltpu.roll(ghost_ref[n, 1, v, at, lanes], amount, 1)
                value = value - (PSEUDO_STEP * DAMPING) * second
                for w in range(variables):
                    value = value + jac_ref[(2 * variables + v) * variables + w] * nearest[w]
                held_ref[n, 0, v, at, lanes] = value
                held_ref[n, 1, v, at, lanes] = part_ref[n, 1, v, at, lanes] - (PSEUDO_STEP * DAMPING) * nearest[v]

    count = rows // parts
    for n in range(instances):
        for part in range(parts):
            for t in range(part * count // SUB, (part + 1) * count // SUB):
                tile(n, t)
            at = pl.ds(part * count, count)
            copies.append(
                pltpu.make_async_copy(
                    held_ref.at[n, :, :, at], out_ref.at[n, pl.ds(0, 2), :, at], sems.at[n, part]
                )
            )
            copies[-1].start()
    for copy in copies:
        copy.wait()


def add_ghosts(part, ghosts, shift, jac):
    instances, layers = part.shape[:2]
    parts = 2
    smem, vmem = (pl.BlockSpec(memory_space=space) for space in (pltpu.SMEM, pltpu.VMEM))
    return pl.pallas_call(
        functools.partial(ghosts_kernel, parts),
        out_shape=jax.ShapeDtypeStruct(part.shape, part.dtype),
        in_specs=[smem, smem, vmem, vmem],
        out_specs=pl.BlockSpec(memory_space=pltpu.HBM),
        scratch_shapes=[
            pltpu.VMEM((instances, 2) + part.shape[2:], part.dtype),
            pltpu.SemaphoreType.DMA((instances, layers - 2)),
            pltpu.SemaphoreType.DMA((instances, parts)),
        ],
        compiler_params=pltpu.CompilerParams(vmem_limit_bytes=12 * MIB),
        cost_estimate=pl.CostEstimate(
            flops=20 * ghosts.size, bytes_accessed=12 * ghosts.size, transcendentals=0
        ),
        name="add_ghosts",
    )(shift, jac, part, pltpu.with_memory_space_constraint(ghosts, pltpu.VMEM))


def on_device(flow, rotor, jacobians, rotor_shift):
    sectors = lax.axis_size("sector")
    sector = lax.axis_index("sector")
    radial = lax.axis_index("radial")
    instances, layers, variables, rows, width = flow.shape

    order = list(ORDER) if sorted(ORDER) == list(range(sectors)) else list(range(sectors))
    slots = [order.index(s) for s in range(sectors)]
    held = lax.all_to_all(rotor.reshape(sectors, -1, width), "sector", 0, 0, axis_index_groups=[order])

    to_right = D2 * flow[0] - D1 * flow[1]
    to_left = D3 * flow[1] - D2 * flow[0]
    r1 = lax.ppermute(to_right, "instance", ring("instance", 1))
    l1 = lax.ppermute(to_left, "instance", ring("instance", -1))

    before = lax.ppermute(flow[..., width - 2 :].swapaxes(3, 4), "sector", ring("sector", 1))
    after = lax.ppermute(flow[..., :2].swapaxes(3, 4), "sector", ring("sector", -1))
    rim = jnp.where(radial == 0, flow[:, :, :, rows - 2 :], flow[:, :, :, :2])
    rim = lax.ppermute(rim, "radial", ring("radial", 1))

    held, r1, l1, before, after, rim = lax.optimization_barrier((held, r1, l1, before, after, rim))
    r2 = lax.ppermute(r1, "instance", ring("instance", 1))
    l2 = lax.ppermute(l1, "instance", ring("instance", -1))
    own_shift = lax.dynamic_slice_in_dim(rotor_shift, jnp.asarray(slots)[sector] * instances // sectors, 1)
    table = jnp.concatenate([own_shift, jnp.asarray(order + slots, jnp.int32)])
    ghosts = lax.all_to_all(turn_annulus(held, table), "sector", 0, 0, axis_index_groups=[order])
    ghosts = ghosts.reshape(rotor.shape)

    middle = jnp.zeros(flow.shape[:-1] + (LANE - 4,), flow.dtype)
    side = jnp.concatenate([after.swapaxes(3, 4), middle, before.swapaxes(3, 4)], -1)
    low = jnp.pad(jnp.where(radial == 0, 0.0, rim), ((0, 0),) * 3 + ((SUB - 2, 0), (0, 0)))
    high = jnp.pad(jnp.where(radial == 0, rim, 0.0), ((0, 0),) * 3 + ((0, SUB - 2), (0, 0)))
    jac = jacobians.reshape(-1) * (0.5 * PSEUDO_STEP)
    part = interior(flow, side, low, high, (r1, l1), jac)
    far = jnp.stack([row[3] * r2 + row[4] * l2 for row in SOURCE])
    part = part - (PSEUDO_STEP * FREQUENCY) * far
    return add_ghosts(part, ghosts, rotor_shift, jac)


def solution(mesh):
    return jax.shard_map(
        on_device,
        mesh=mesh,
        in_specs=(
            P("instance", None, None, "radial", "sector"),
            P("instance", None, None, "radial", "sector"),
            P(),
            P("instance"),
        ),
        out_specs=P("instance", None, None, "radial", "sector"),
        check_vma=False,
    )
```

```python
import functools
import math

import jax
import jax.numpy as jnp
from jax import lax
from jax.experimental import pallas as pl
from jax.experimental.pallas import tpu as pltpu
from jax.sharding import PartitionSpec as P

PSEUDO_STEP = 0.25
DAMPING = 0.0625
FREQUENCY = 0.5

D1 = 0.5 / math.tan(math.pi / 8)
D2 = 0.5
D3 = 0.5 / math.tan(3 * math.pi / 8)

SOURCE = ((D1, 1.0, 1.0, D3, D3), (-D1, -2 * D3, -2 * D1, -2 * D3 * D3, -0.5))

ORDER = (
    22, 7, 8, 24, 31, 1, 28, 17, 27, 15, 19, 23, 0, 21, 4, 11,
    9, 29, 13, 5, 14, 26, 25, 3, 12, 20, 2, 6, 30, 10, 16, 18,
)

SUB, LANE = 8, 128
MIB = 1024 * 1024


def ring(axis, distance):
    size = lax.axis_size(axis)
    return [(i, (i + distance) % size) for i in range(size)]


def turn_kernel(parts, order, table_ref, x_ref, y_ref, held_ref, sems):
    blocks, rows, width = x_ref.shape
    halves = width // LANE
    strips = blocks * halves
    whole = table_ref[0] // LANE
    kept = lax.broadcasted_iota(jnp.int32, (rows, LANE), 1) < LANE - table_ref[0] % LANE

    def strip(index):
        at = pl.multiple_of(lax.bitwise_and(index, halves - 1) * LANE, LANE)
        block = table_ref[1 + lax.shift_right_logical(index, halves.bit_length() - 1)]
        return x_ref[block, :, pl.ds(at, LANE)]

    def fill(slot):
        first = order[slot] * halves + strips - 1 - whole
        before = strip(lax.bitwise_and(first, strips - 1))
        for h in range(halves):
            current = strip(lax.bitwise_and(first + h + 1, strips - 1))
            held_ref[slot, :, h * LANE : (h + 1) * LANE] = jnp.where(kept, current, before)
            before = current

    copies = []
    for part in range(parts):
        first, count = part * (blocks // parts), blocks // parts
        for slot in range(first, first + count):
            fill(slot)
        at = pl.ds(first, count)
        copies.append(pltpu.make_async_copy(held_ref.at[at], y_ref.at[at], sems.at[part]))
        copies[-1].start()
    for copy in copies:
        copy.wait()


def turn_annulus(x, table, order):
    parts = 4
    return pl.pallas_call(
        functools.partial(turn_kernel, parts, order),
        out_shape=pltpu.HBM(x.shape, x.dtype),
        in_specs=[
            pl.BlockSpec(memory_space=pltpu.SMEM),
            pl.BlockSpec(memory_space=pltpu.VMEM),
        ],
        out_specs=pl.BlockSpec(memory_space=pltpu.HBM),
        scratch_shapes=[pltpu.VMEM(x.shape, x.dtype), pltpu.SemaphoreType.DMA((parts,))],
        compiler_params=pltpu.CompilerParams(vmem_limit_bytes=8 * MIB),
        cost_estimate=pl.CostEstimate(flops=x.size, bytes_accessed=8 * x.size, transcendentals=0),
        name="turn_annulus",
    )(table, x)


def interior_kernel(
    jac_ref, u_ref, side_ref, low_ref, high_ref,
    r1_ref, l1_ref, out_ref, first_ref, fourth_ref,
):
    instances, layers, variables, rows, width = u_ref.shape
    lane = lax.broadcasted_iota(jnp.int32, (rows, LANE), 1)
    sub = lax.broadcasted_iota(jnp.int32, (SUB, width), 0)
    for n in range(instances):
        for layer in range(layers):
            for w in range(variables):
                u = u_ref[n, layer, w]
                side = side_ref[n, layer, w]
                low8, high8 = low_ref[n, layer, w], high_ref[n, layer, w]

                def left(k):
                    rim = jnp.where(lane >= LANE - k, side, u[:, width - LANE :])
                    return pltpu.roll(jnp.concatenate([u[:, : width - LANE], rim], 1), k, 1)

                def right(k):
                    rim = jnp.where(lane < k, side, u[:, :LANE])
                    return pltpu.roll(jnp.concatenate([rim, u[:, LANE:]], 1), width - k, 1)

                def low(k):
                    rim = jnp.where(sub >= SUB - k, low8, u[rows - SUB :])
                    return pltpu.roll(jnp.concatenate([u[: rows - SUB], rim], 0), k, 0)

                def high(k):
                    rim = jnp.where(sub < k, high8, u[:SUB])
                    return pltpu.roll(jnp.concatenate([rim, u[SUB:]], 0), rows - k, 0)

                left1, right1, low1, high1 = left(1), right(1), low(1), high(1)
                near = left1 + right1 + (low1 + high1)
                far = left(2) + right(2) + (low(2) + high(2))
                next1 = u_ref[n, min(layer + 1, layers - 1), w]
                next2 = u_ref[n, min(layer + 2, layers - 1), w]
                near, far = near + next1, far + next2
                axial = next1
                if layer >= 1:
                    previous = u_ref[n, layer - 1, w]
                    near, axial = near + previous, axial - previous
                if layer >= 2:
                    far = far + u_ref[n, layer - 2, w]
                first_ref[w] = right1 - left1
                first_ref[variables + w] = high1 - low1
                first_ref[2 * variables + w] = axial
                fourth_ref[w] = far - 4.0 * near + 18.0 * u

            def tile(t, carry):
                at = pl.ds(pl.multiple_of(t * SUB, SUB), SUB)
                firsts = [first_ref[k, at] for k in range(3 * variables)]
                for v in range(variables):
                    value = u_ref[n, layer, v, at] - (PSEUDO_STEP * DAMPING) * fourth_ref[v, at]
                    source = SOURCE[n][0] * u_ref[1 - n, layer, v, at]
                    for k, ref in enumerate((r1_ref, l1_ref)):
                        source = source + SOURCE[n][k + 1] * ref[layer, v, at]
                    value = value - (PSEUDO_STEP * FREQUENCY) * source
                    for d in range(3):
                        for w in range(variables):
                            k = (d * variables + v) * variables + w
                            value = value - jac_ref[k] * firsts[d * variables + w]
                    out_ref[n, layer, v, at] = value
                return carry

            lax.fori_loop(0, rows // SUB, tile, 0)


def interior(flow, side, low, high, received, jac):
    variables, rows, width = flow.shape[2:]
    whole = pl.BlockSpec(memory_space=pltpu.VMEM)
    return pl.pallas_call(
        interior_kernel,
        out_shape=jax.ShapeDtypeStruct(flow.shape, flow.dtype),
        in_specs=[pl.BlockSpec(memory_space=pltpu.SMEM)] + [whole] * 6,
        out_specs=whole,
        scratch_shapes=[
            pltpu.VMEM((3 * variables, rows, width), jnp.float32),
            pltpu.VMEM((variables, rows, width), jnp.float32),
        ],
        compiler_params=pltpu.CompilerParams(vmem_limit_bytes=24 * MIB),
        cost_estimate=pl.CostEstimate(
            flops=80 * flow.size, bytes_accessed=20 * flow.size, transcendentals=0
        ),
        name="interior",
    )(jac, flow, side, low, high, *received)


def ghosts_kernel(parts, shift_ref, jac_ref, part_ref, ghost_ref, out_ref, held_ref, last_sems, sems):
    instances, layers, variables, rows, width = part_ref.shape
    copies = []
    for n in range(instances):
        for layer in range(2, layers):
            copies.append(
                pltpu.make_async_copy(part_ref.at[n, layer], out_ref.at[n, layer], last_sems.at[n, layer - 2])
            )
            copies[-1].start()

    def tile(n, t):
        amount = shift_ref[n] % LANE
        at = pl.ds(pl.multiple_of(t * SUB, SUB), SUB)
        for first in range(0, width, LANE):
            lanes = slice(first, first + LANE)
            nearest = [pltpu.roll(ghost_ref[n, 0, w, at, lanes], amount, 1) for w in range(variables)]
            for v in range(variables):
                value = part_ref[n, 0, v, at, lanes] + (4.0 * PSEUDO_STEP * DAMPING) * nearest[v]
                second = pltpu.roll(ghost_ref[n, 1, v, at, lanes], amount, 1)
                value = value - (PSEUDO_STEP * DAMPING) * second
                for w in range(variables):
                    value = value + jac_ref[(2 * variables + v) * variables + w] * nearest[w]
                held_ref[n, 0, v, at, lanes] = value
                held_ref[n, 1, v, at, lanes] = part_ref[n, 1, v, at, lanes] - (PSEUDO_STEP * DAMPING) * nearest[v]

    count = rows // parts
    for n in range(instances):
        for part in range(parts):
            for t in range(part * count // SUB, (part + 1) * count // SUB):
                tile(n, t)
            at = pl.ds(part * count, count)
            copies.append(
                pltpu.make_async_copy(
                    held_ref.at[n, :, :, at], out_ref.at[n, pl.ds(0, 2), :, at], sems.at[n, part]
                )
            )
            copies[-1].start()
    for copy in copies:
        copy.wait()


def add_ghosts(part, ghosts, shift, jac):
    instances, layers = part.shape[:2]
    parts = 2
    smem, vmem = (pl.BlockSpec(memory_space=space) for space in (pltpu.SMEM, pltpu.VMEM))
    return pl.pallas_call(
        functools.partial(ghosts_kernel, parts),
        out_shape=jax.ShapeDtypeStruct(part.shape, part.dtype),
        in_specs=[smem, smem, vmem, vmem],
        out_specs=pl.BlockSpec(memory_space=pltpu.HBM),
        scratch_shapes=[
            pltpu.VMEM((instances, 2) + part.shape[2:], part.dtype),
            pltpu.SemaphoreType.DMA((instances, layers - 2)),
            pltpu.SemaphoreType.DMA((instances, parts)),
        ],
        compiler_params=pltpu.CompilerParams(vmem_limit_bytes=12 * MIB),
        cost_estimate=pl.CostEstimate(
            flops=20 * ghosts.size, bytes_accessed=12 * ghosts.size, transcendentals=0
        ),
        name="add_ghosts",
    )(shift, jac, part, pltpu.with_memory_space_constraint(ghosts, pltpu.VMEM))


def on_device(flow, rotor, jacobians, rotor_shift):
    sectors = lax.axis_size("sector")
    sector = lax.axis_index("sector")
    radial = lax.axis_index("radial")
    instances, layers, variables, rows, width = flow.shape

    order = list(ORDER) if sorted(ORDER) == list(range(sectors)) else list(range(sectors))
    slots = [order.index(s) for s in range(sectors)]
    held = lax.all_to_all(rotor.reshape(sectors, -1, width), "sector", 0, 0, axis_index_groups=[order])

    to_right = D2 * flow[0] - D1 * flow[1]
    to_left = D3 * flow[1] - D2 * flow[0]
    r1 = lax.ppermute(to_right, "instance", ring("instance", 1))
    l1 = lax.ppermute(to_left, "instance", ring("instance", -1))

    before = lax.ppermute(flow[..., width - 2 :].swapaxes(3, 4), "sector", ring("sector", 1))
    after = lax.ppermute(flow[..., :2].swapaxes(3, 4), "sector", ring("sector", -1))
    rim = jnp.where(radial == 0, flow[:, :, :, rows - 2 :], flow[:, :, :, :2])
    rim = lax.ppermute(rim, "radial", ring("radial", 1))

    held, r1, l1, before, after, rim = lax.optimization_barrier((held, r1, l1, before, after, rim))
    r2 = lax.ppermute(r1, "instance", ring("instance", 1))
    l2 = lax.ppermute(l1, "instance", ring("instance", -1))
    own_shift = lax.dynamic_slice_in_dim(rotor_shift, jnp.asarray(slots)[sector] * instances // sectors, 1)
    table = jnp.concatenate([own_shift, jnp.asarray(slots, jnp.int32)])
    ghosts = lax.all_to_all(turn_annulus(held, table, order), "sector", 0, 0, axis_index_groups=[order])
    ghosts = ghosts.reshape(rotor.shape)

    middle = jnp.zeros(flow.shape[:-1] + (LANE - 4,), flow.dtype)
    side = jnp.concatenate([after.swapaxes(3, 4), middle, before.swapaxes(3, 4)], -1)
    low = jnp.pad(jnp.where(radial == 0, 0.0, rim), ((0, 0),) * 3 + ((SUB - 2, 0), (0, 0)))
    high = jnp.pad(jnp.where(radial == 0, rim, 0.0), ((0, 0),) * 3 + ((0, SUB - 2), (0, 0)))
    jac = jacobians.reshape(-1) * (0.5 * PSEUDO_STEP)
    part = interior(flow, side, low, high, (r1, l1), jac)
    far = jnp.stack([row[3] * r2 + row[4] * l2 for row in SOURCE])
    part = part - (PSEUDO_STEP * FREQUENCY) * far
    return add_ghosts(part, ghosts, rotor_shift, jac)


def solution(mesh):
    return jax.shard_map(
        on_device,
        mesh=mesh,
        in_specs=(
            P("instance", None, None, "radial", "sector"),
            P("instance", None, None, "radial", "sector"),
            P(),
            P("instance"),
        ),
        out_specs=P("instance", None, None, "radial", "sector"),
        check_vma=False,
    )
```

```python
import functools
import math

import jax
import jax.numpy as jnp
from jax import lax
from jax.experimental import pallas as pl
from jax.experimental.pallas import tpu as pltpu
from jax.sharding import PartitionSpec as P

PSEUDO_STEP = 0.25
DAMPING = 0.0625
FREQUENCY = 0.5

D1 = 0.5 / math.tan(math.pi / 8)
D2 = 0.5
D3 = 0.5 / math.tan(3 * math.pi / 8)

SOURCE = ((D1, 1.0, 1.0, D3, D3), (-D1, -2 * D3, -2 * D1, -2 * D3 * D3, -0.5))

ORDER = (
    22, 7, 8, 24, 31, 1, 28, 17, 27, 15, 19, 23, 0, 21, 4, 11,
    9, 29, 13, 5, 14, 26, 25, 3, 12, 20, 2, 6, 30, 10, 16, 18,
)

SUB, LANE = 8, 128
MIB = 1024 * 1024


def ring(axis, distance):
    size = lax.axis_size(axis)
    return [(i, (i + distance) % size) for i in range(size)]


def turn_kernel(parts, order, table_ref, x_ref, y_ref, held_ref, sems):
    blocks, rows, width = x_ref.shape
    halves = width // LANE
    strips = blocks * halves
    whole = table_ref[0] // LANE
    kept = lax.broadcasted_iota(jnp.int32, (rows, LANE), 1) < LANE - table_ref[0] % LANE

    def strip(index):
        at = pl.multiple_of(lax.bitwise_and(index, halves - 1) * LANE, LANE)
        block = table_ref[1 + lax.shift_right_logical(index, halves.bit_length() - 1)]
        return x_ref[block, :, pl.ds(at, LANE)]

    def fill(slot):
        first = order[slot] * halves + strips - 1 - whole
        before = strip(lax.bitwise_and(first, strips - 1))
        for h in range(halves):
            current = strip(lax.bitwise_and(first + h + 1, strips - 1))
            held_ref[slot, :, h * LANE : (h + 1) * LANE] = jnp.where(kept, current, before)
            before = current

    copies = []
    for part in range(parts):
        first, count = part * (blocks // parts), blocks // parts
        for slot in range(first, first + count):
            fill(slot)
        at = pl.ds(first, count)
        copies.append(pltpu.make_async_copy(held_ref.at[at], y_ref.at[at], sems.at[part]))
        copies[-1].start()
    for copy in copies:
        copy.wait()


def turn_annulus(x, table, order):
    parts = 8
    return pl.pallas_call(
        functools.partial(turn_kernel, parts, order),
        out_shape=pltpu.HBM(x.shape, x.dtype),
        in_specs=[
            pl.BlockSpec(memory_space=pltpu.SMEM),
            pl.BlockSpec(memory_space=pltpu.VMEM),
        ],
        out_specs=pl.BlockSpec(memory_space=pltpu.HBM),
        scratch_shapes=[pltpu.VMEM(x.shape, x.dtype), pltpu.SemaphoreType.DMA((parts,))],
        compiler_params=pltpu.CompilerParams(vmem_limit_bytes=8 * MIB),
        cost_estimate=pl.CostEstimate(flops=x.size, bytes_accessed=8 * x.size, transcendentals=0),
        name="turn_annulus",
    )(table, x)


def interior_kernel(
    jac_ref, u_ref, side_ref, low_ref, high_ref,
    r1_ref, l1_ref, out_ref, first_ref, fourth_ref,
):
    instances, layers, variables, rows, width = u_ref.shape
    lane = lax.broadcasted_iota(jnp.int32, (rows, LANE), 1)
    sub = lax.broadcasted_iota(jnp.int32, (SUB, width), 0)
    for n in range(instances):
        for layer in range(layers):
            for w in range(variables):
                u = u_ref[n, layer, w]
                side = side_ref[n, layer, w]
                low8, high8 = low_ref[n, layer, w], high_ref[n, layer, w]

                def left(k):
                    rim = jnp.where(lane >= LANE - k, side, u[:, width - LANE :])
                    return pltpu.roll(jnp.concatenate([u[:, : width - LANE], rim], 1), k, 1)

                def right(k):
                    rim = jnp.where(lane < k, side, u[:, :LANE])
                    return pltpu.roll(jnp.concatenate([rim, u[:, LANE:]], 1), width - k, 1)

                def low(k):
                    rim = jnp.where(sub >= SUB - k, low8, u[rows - SUB :])
                    return pltpu.roll(jnp.concatenate([u[: rows - SUB], rim], 0), k, 0)

                def high(k):
                    rim = jnp.where(sub < k, high8, u[:SUB])
                    return pltpu.roll(jnp.concatenate([rim, u[SUB:]], 0), rows - k, 0)

                left1, right1, low1, high1 = left(1), right(1), low(1), high(1)
                near = left1 + right1 + (low1 + high1)
                far = left(2) + right(2) + (low(2) + high(2))
                next1 = u_ref[n, min(layer + 1, layers - 1), w]
                next2 = u_ref[n, min(layer + 2, layers - 1), w]
                near, far = near + next1, far + next2
                axial = next1
                if layer >= 1:
                    previous = u_ref[n, layer - 1, w]
                    near, axial = near + previous, axial - previous
                if layer >= 2:
                    far = far + u_ref[n, layer - 2, w]
                first_ref[w] = right1 - left1
                first_ref[variables + w] = high1 - low1
                first_ref[2 * variables + w] = axial
                fourth_ref[w] = far - 4.0 * near + 18.0 * u

            def tile(t, carry):
                at = pl.ds(pl.multiple_of(t * SUB, SUB), SUB)
                firsts = [first_ref[k, at] for k in range(3 * variables)]
                for v in range(variables):
                    value = u_ref[n, layer, v, at] - (PSEUDO_STEP * DAMPING) * fourth_ref[v, at]
                    source = SOURCE[n][0] * u_ref[1 - n, layer, v, at]
                    for k, ref in enumerate((r1_ref, l1_ref)):
                        source = source + SOURCE[n][k + 1] * ref[layer, v, at]
                    value = value - (PSEUDO_STEP * FREQUENCY) * source
                    for d in range(3):
                        for w in range(variables):
                            k = (d * variables + v) * variables + w
                            value = value - jac_ref[k] * firsts[d * variables + w]
                    out_ref[n, layer, v, at] = value
                return carry

            lax.fori_loop(0, rows // SUB, tile, 0)


def interior(flow, side, low, high, received, jac):
    variables, rows, width = flow.shape[2:]
    whole = pl.BlockSpec(memory_space=pltpu.VMEM)
    return pl.pallas_call(
        interior_kernel,
        out_shape=jax.ShapeDtypeStruct(flow.shape, flow.dtype),
        in_specs=[pl.BlockSpec(memory_space=pltpu.SMEM)] + [whole] * 6,
        out_specs=whole,
        scratch_shapes=[
            pltpu.VMEM((3 * variables, rows, width), jnp.float32),
            pltpu.VMEM((variables, rows, width), jnp.float32),
        ],
        compiler_params=pltpu.CompilerParams(vmem_limit_bytes=24 * MIB),
        cost_estimate=pl.CostEstimate(
            flops=80 * flow.size, bytes_accessed=20 * flow.size, transcendentals=0
        ),
        name="interior",
    )(jac, flow, side, low, high, *received)


def ghosts_kernel(parts, shift_ref, axial_ref, part_ref, ghost_ref, out_ref, held_ref, last_sems, sems):
    instances, layers, variables, rows, width = part_ref.shape
    copies = []
    for n in range(instances):
        for layer in range(2, layers):
            copies.append(
                pltpu.make_async_copy(part_ref.at[n, layer], out_ref.at[n, layer], last_sems.at[n, layer - 2])
            )
            copies[-1].start()

    def tile(n, t):
        amount = shift_ref[n] % LANE
        at = pl.ds(pl.multiple_of(t * SUB, SUB), SUB)
        for first in range(0, width, LANE):
            lanes = slice(first, first + LANE)
            nearest = [pltpu.roll(ghost_ref[n, 0, w, at, lanes], amount, 1) for w in range(variables)]
            for v in range(variables):
                value = part_ref[n, 0, v, at, lanes]
                second = pltpu.roll(ghost_ref[n, 1, v, at, lanes], amount, 1)
                value = value - (PSEUDO_STEP * DAMPING) * second
                for w in range(variables):
                    value = value + axial_ref[v * variables + w] * nearest[w]
                held_ref[n, 0, v, at, lanes] = value
                held_ref[n, 1, v, at, lanes] = part_ref[n, 1, v, at, lanes] - (PSEUDO_STEP * DAMPING) * nearest[v]

    count = rows // parts
    for n in range(instances):
        for part in range(parts):
            for t in range(part * count // SUB, (part + 1) * count // SUB):
                tile(n, t)
            at = pl.ds(part * count, count)
            copies.append(
                pltpu.make_async_copy(
                    held_ref.at[n, :, :, at], out_ref.at[n, pl.ds(0, 2), :, at], sems.at[n, part]
                )
            )
            copies[-1].start()
    for copy in copies:
        copy.wait()


def add_ghosts(part, ghosts, shift, axial):
    instances, layers = part.shape[:2]
    parts = 2
    smem, vmem = (pl.BlockSpec(memory_space=space) for space in (pltpu.SMEM, pltpu.VMEM))
    return pl.pallas_call(
        functools.partial(ghosts_kernel, parts),
        out_shape=jax.ShapeDtypeStruct(part.shape, part.dtype),
        in_specs=[smem, smem, vmem, vmem],
        out_specs=pl.BlockSpec(memory_space=pltpu.HBM),
        scratch_shapes=[
            pltpu.VMEM((instances, 2) + part.shape[2:], part.dtype),
            pltpu.SemaphoreType.DMA((instances, layers - 2)),
            pltpu.SemaphoreType.DMA((instances, parts)),
        ],
        compiler_params=pltpu.CompilerParams(vmem_limit_bytes=12 * MIB),
        cost_estimate=pl.CostEstimate(
            flops=20 * ghosts.size, bytes_accessed=12 * ghosts.size, transcendentals=0
        ),
        name="add_ghosts",
    )(shift, axial, part, pltpu.with_memory_space_constraint(ghosts, pltpu.VMEM))


def on_device(flow, rotor, jacobians, rotor_shift):
    sectors = lax.axis_size("sector")
    sector = lax.axis_index("sector")
    radial = lax.axis_index("radial")
    instances, layers, variables, rows, width = flow.shape

    order = list(ORDER) if sorted(ORDER) == list(range(sectors)) else list(range(sectors))
    slots = [order.index(s) for s in range(sectors)]
    held = lax.all_to_all(rotor.reshape(sectors, -1, width), "sector", 0, 0, axis_index_groups=[order])

    to_right = D2 * flow[0] - D1 * flow[1]
    to_left = D3 * flow[1] - D2 * flow[0]
    r1 = lax.ppermute(to_right, "instance", ring("instance", 1))
    l1 = lax.ppermute(to_left, "instance", ring("instance", -1))

    before = lax.ppermute(flow[..., width - 2 :].swapaxes(3, 4), "sector", ring("sector", 1))
    after = lax.ppermute(flow[..., :2].swapaxes(3, 4), "sector", ring("sector", -1))
    rim = jnp.where(radial == 0, flow[:, :, :, rows - 2 :], flow[:, :, :, :2])
    rim = lax.ppermute(rim, "radial", ring("radial", 1))

    held, r1, l1, before, after, rim = lax.optimization_barrier((held, r1, l1, before, after, rim))
    r2 = lax.ppermute(r1, "instance", ring("instance", 1))
    l2 = lax.ppermute(l1, "instance", ring("instance", -1))
    own_shift = lax.dynamic_slice_in_dim(rotor_shift, jnp.asarray(slots)[sector] * instances // sectors, 1)
    table = jnp.concatenate([own_shift, jnp.asarray(slots, jnp.int32)])
    ghosts = lax.all_to_all(turn_annulus(held, table, order), "sector", 0, 0, axis_index_groups=[order])
    ghosts = ghosts.reshape(rotor.shape)

    middle = jnp.zeros(flow.shape[:-1] + (LANE - 4,), flow.dtype)
    side = jnp.concatenate([after.swapaxes(3, 4), middle, before.swapaxes(3, 4)], -1)
    low = jnp.pad(jnp.where(radial == 0, 0.0, rim), ((0, 0),) * 3 + ((SUB - 2, 0), (0, 0)))
    high = jnp.pad(jnp.where(radial == 0, rim, 0.0), ((0, 0),) * 3 + ((0, SUB - 2), (0, 0)))
    jac = jacobians.reshape(-1) * (0.5 * PSEUDO_STEP)
    part = interior(flow, side, low, high, (r1, l1), jac)
    far = jnp.stack([row[3] * r2 + row[4] * l2 for row in SOURCE])
    part = part - (PSEUDO_STEP * FREQUENCY) * far
    axial = jacobians[2] * (0.5 * PSEUDO_STEP) + (4.0 * PSEUDO_STEP * DAMPING) * jnp.eye(variables)
    return add_ghosts(part, ghosts, rotor_shift, axial.reshape(-1))


def solution(mesh):
    return jax.shard_map(
        on_device,
        mesh=mesh,
        in_specs=(
            P("instance", None, None, "radial", "sector"),
            P("instance", None, None, "radial", "sector"),
            P(),
            P("instance"),
        ),
        out_specs=P("instance", None, None, "radial", "sector"),
        check_vma=False,
    )
```

```python
import functools
import math

import jax
import jax.numpy as jnp
from jax import lax
from jax.experimental import pallas as pl
from jax.experimental.pallas import tpu as pltpu
from jax.sharding import PartitionSpec as P

PSEUDO_STEP = 0.25
DAMPING = 0.0625
FREQUENCY = 0.5

D1 = 0.5 / math.tan(math.pi / 8)
D2 = 0.5
D3 = 0.5 / math.tan(3 * math.pi / 8)

SOURCE = ((D1, 1.0, 1.0, D3, D3), (-D1, -2 * D3, -2 * D1, -2 * D3 * D3, -0.5))

ORDER = (
    22, 7, 8, 24, 31, 1, 28, 17, 27, 15, 19, 23, 0, 21, 4, 11,
    9, 29, 13, 5, 14, 26, 25, 3, 12, 20, 2, 6, 30, 10, 16, 18,
)

SUB, LANE = 8, 128
MIB = 1024 * 1024


def ring(axis, distance):
    size = lax.axis_size(axis)
    return [(i, (i + distance) % size) for i in range(size)]


def turn_kernel(parts, order, table_ref, x_ref, y_ref, held_ref, sems):
    blocks, rows, width = x_ref.shape
    halves = width // LANE
    strips = blocks * halves
    whole = table_ref[0] // LANE
    kept = lax.broadcasted_iota(jnp.int32, (rows, LANE), 1) < LANE - table_ref[0] % LANE

    def strip(index):
        at = pl.multiple_of(lax.bitwise_and(index, halves - 1) * LANE, LANE)
        block = table_ref[1 + lax.shift_right_logical(index, halves.bit_length() - 1)]
        return x_ref[block, :, pl.ds(at, LANE)]

    def fill(slot):
        first = order[slot] * halves + strips - 1 - whole
        before = strip(lax.bitwise_and(first, strips - 1))
        for h in range(halves):
            current = strip(lax.bitwise_and(first + h + 1, strips - 1))
            held_ref[slot, :, h * LANE : (h + 1) * LANE] = jnp.where(kept, current, before)
            before = current

    copies = []
    for part in range(parts):
        first, count = part * (blocks // parts), blocks // parts
        for slot in range(first, first + count):
            fill(slot)
        at = pl.ds(first, count)
        copies.append(pltpu.make_async_copy(held_ref.at[at], y_ref.at[at], sems.at[part]))
        copies[-1].start()
    for copy in copies:
        copy.wait()


def turn_annulus(x, table, order):
    parts = 8
    return pl.pallas_call(
        functools.partial(turn_kernel, parts, order),
        out_shape=pltpu.HBM(x.shape, x.dtype),
        in_specs=[
            pl.BlockSpec(memory_space=pltpu.SMEM),
            pl.BlockSpec(memory_space=pltpu.VMEM),
        ],
        out_specs=pl.BlockSpec(memory_space=pltpu.HBM),
        scratch_shapes=[pltpu.VMEM(x.shape, x.dtype), pltpu.SemaphoreType.DMA((parts,))],
        compiler_params=pltpu.CompilerParams(vmem_limit_bytes=8 * MIB),
        cost_estimate=pl.CostEstimate(flops=x.size, bytes_accessed=8 * x.size, transcendentals=0),
        name="turn_annulus",
    )(table, x)


def interior_kernel(
    jac_ref, u_ref, side_ref, low_ref, high_ref,
    r1_ref, l1_ref, out_ref, first_ref, fourth_ref,
):
    instances, layers, variables, rows, width = u_ref.shape
    lane = lax.broadcasted_iota(jnp.int32, (rows, LANE), 1)
    sub = lax.broadcasted_iota(jnp.int32, (SUB, width), 0)
    for n in range(instances):
        for layer in range(layers):
            for w in range(variables):
                u = u_ref[n, layer, w]
                side = side_ref[n, layer, w]
                low8, high8 = low_ref[n, layer, w], high_ref[n, layer, w]

                def left(k):
                    rim = jnp.where(lane >= LANE - k, side, u[:, width - LANE :])
                    return pltpu.roll(jnp.concatenate([u[:, : width - LANE], rim], 1), k, 1)

                def right(k):
                    rim = jnp.where(lane < k, side, u[:, :LANE])
                    return pltpu.roll(jnp.concatenate([rim, u[:, LANE:]], 1), width - k, 1)

                def low(k):
                    rim = jnp.where(sub >= SUB - k, low8, u[rows - SUB :])
                    return pltpu.roll(jnp.concatenate([u[: rows - SUB], rim], 0), k, 0)

                def high(k):
                    rim = jnp.where(sub < k, high8, u[:SUB])
                    return pltpu.roll(jnp.concatenate([rim, u[SUB:]], 0), rows - k, 0)

                left1, right1, low1, high1 = left(1), right(1), low(1), high(1)
                near = left1 + right1 + (low1 + high1)
                far = left(2) + right(2) + (low(2) + high(2))
                next1 = u_ref[n, min(layer + 1, layers - 1), w]
                next2 = u_ref[n, min(layer + 2, layers - 1), w]
                near, far = near + next1, far + next2
                axial = next1
                if layer >= 1:
                    previous = u_ref[n, layer - 1, w]
                    near, axial = near + previous, axial - previous
                if layer >= 2:
                    far = far + u_ref[n, layer - 2, w]
                first_ref[w] = right1 - left1
                first_ref[variables + w] = high1 - low1
                first_ref[2 * variables + w] = axial
                fourth_ref[w] = far - 4.0 * near + 18.0 * u

            def tile(t, carry):
                at = pl.ds(pl.multiple_of(t * SUB, SUB), SUB)
                firsts = [first_ref[k, at] for k in range(3 * variables)]
                for v in range(variables):
                    value = u_ref[n, layer, v, at] - (PSEUDO_STEP * DAMPING) * fourth_ref[v, at]
                    source = SOURCE[n][0] * u_ref[1 - n, layer, v, at]
                    for k, ref in enumerate((r1_ref, l1_ref)):
                        source = source + SOURCE[n][k + 1] * ref[layer, v, at]
                    value = value - (PSEUDO_STEP * FREQUENCY) * source
                    for d in range(3):
                        for w in range(variables):
                            k = (d * variables + v) * variables + w
                            value = value - jac_ref[k] * firsts[d * variables + w]
                    out_ref[n, layer, v, at] = value
                return carry

            lax.fori_loop(0, rows // SUB, tile, 0)


def interior(flow, side, low, high, received, jac):
    variables, rows, width = flow.shape[2:]
    whole = pl.BlockSpec(memory_space=pltpu.VMEM)
    return pl.pallas_call(
        interior_kernel,
        out_shape=jax.ShapeDtypeStruct(flow.shape, flow.dtype),
        in_specs=[pl.BlockSpec(memory_space=pltpu.SMEM)] + [whole] * 6,
        out_specs=whole,
        scratch_shapes=[
            pltpu.VMEM((3 * variables, rows, width), jnp.float32),
            pltpu.VMEM((variables, rows, width), jnp.float32),
        ],
        compiler_params=pltpu.CompilerParams(vmem_limit_bytes=24 * MIB),
        cost_estimate=pl.CostEstimate(
            flops=80 * flow.size, bytes_accessed=20 * flow.size, transcendentals=0
        ),
        name="interior",
    )(jac, flow, side, low, high, *received)


def far_layers_kernel(part_ref, out_ref, sems):
    copies = []
    for n in range(part_ref.shape[0]):
        at = pl.ds(2, part_ref.shape[1] - 2)
        copies.append(pltpu.make_async_copy(part_ref.at[n, at], out_ref.at[n, at], sems.at[n]))
        copies[-1].start()
    for copy in copies:
        copy.wait()


def far_layers(part):
    return pl.pallas_call(
        far_layers_kernel,
        out_shape=pltpu.HBM(part.shape, part.dtype),
        in_specs=[pl.BlockSpec(memory_space=pltpu.VMEM)],
        out_specs=pl.BlockSpec(memory_space=pltpu.HBM),
        scratch_shapes=[pltpu.SemaphoreType.DMA((part.shape[0],))],
        compiler_params=pltpu.CompilerParams(vmem_limit_bytes=8 * MIB),
        cost_estimate=pl.CostEstimate(flops=0, bytes_accessed=4 * part.size, transcendentals=0),
        name="far_layers",
    )(part)


def ghosts_kernel(parts, shift_ref, axial_ref, base_ref, part_ref, ghost_ref, out_ref, held_ref, sems):
    instances, _, variables, rows, width = part_ref.shape
    copies = []

    def tile(n, t):
        amount = shift_ref[n] % LANE
        at = pl.ds(pl.multiple_of(t * SUB, SUB), SUB)
        for first in range(0, width, LANE):
            lanes = slice(first, first + LANE)
            nearest = [pltpu.roll(ghost_ref[n, 0, w, at, lanes], amount, 1) for w in range(variables)]
            for v in range(variables):
                value = part_ref[n, 0, v, at, lanes]
                second = pltpu.roll(ghost_ref[n, 1, v, at, lanes], amount, 1)
                value = value - (PSEUDO_STEP * DAMPING) * second
                for w in range(variables):
                    value = value + axial_ref[v * variables + w] * nearest[w]
                held_ref[n, 0, v, at, lanes] = value
                held_ref[n, 1, v, at, lanes] = part_ref[n, 1, v, at, lanes] - (PSEUDO_STEP * DAMPING) * nearest[v]

    count = rows // parts
    for n in range(instances):
        for part in range(parts):
            for t in range(part * count // SUB, (part + 1) * count // SUB):
                tile(n, t)
            at = pl.ds(part * count, count)
            copies.append(
                pltpu.make_async_copy(
                    held_ref.at[n, :, :, at], out_ref.at[n, pl.ds(0, 2), :, at], sems.at[n, part]
                )
            )
            copies[-1].start()
    for copy in copies:
        copy.wait()


def add_ghosts(part, ghosts, shift, axial):
    instances = part.shape[0]
    parts = 2
    smem, vmem = (pl.BlockSpec(memory_space=space) for space in (pltpu.SMEM, pltpu.VMEM))
    return pl.pallas_call(
        functools.partial(ghosts_kernel, parts),
        out_shape=pltpu.HBM(part.shape, part.dtype),
        in_specs=[smem, smem, pl.BlockSpec(memory_space=pltpu.HBM), vmem, vmem],
        input_output_aliases={2: 0},
        out_specs=pl.BlockSpec(memory_space=pltpu.HBM),
        scratch_shapes=[
            pltpu.VMEM((instances, 2) + part.shape[2:], part.dtype),
            pltpu.SemaphoreType.DMA((instances, parts)),
        ],
        compiler_params=pltpu.CompilerParams(vmem_limit_bytes=12 * MIB),
        cost_estimate=pl.CostEstimate(
            flops=20 * ghosts.size, bytes_accessed=12 * ghosts.size, transcendentals=0
        ),
        name="add_ghosts",
    )(shift, axial, far_layers(part), part, pltpu.with_memory_space_constraint(ghosts, pltpu.VMEM))


def on_device(flow, rotor, jacobians, rotor_shift):
    sectors = lax.axis_size("sector")
    sector = lax.axis_index("sector")
    radial = lax.axis_index("radial")
    instances, layers, variables, rows, width = flow.shape

    order = list(ORDER) if sorted(ORDER) == list(range(sectors)) else list(range(sectors))
    slots = [order.index(s) for s in range(sectors)]
    held = lax.all_to_all(rotor.reshape(sectors, -1, width), "sector", 0, 0, axis_index_groups=[order])

    to_right = D2 * flow[0] - D1 * flow[1]
    to_left = D3 * flow[1] - D2 * flow[0]
    r1 = lax.ppermute(to_right, "instance", ring("instance", 1))
    l1 = lax.ppermute(to_left, "instance", ring("instance", -1))

    before = lax.ppermute(flow[..., width - 2 :].swapaxes(3, 4), "sector", ring("sector", 1))
    after = lax.ppermute(flow[..., :2].swapaxes(3, 4), "sector", ring("sector", -1))
    rim = jnp.where(radial == 0, flow[:, :, :, rows - 2 :], flow[:, :, :, :2])
    rim = lax.ppermute(rim, "radial", ring("radial", 1))

    held, r1, l1, before, after, rim = lax.optimization_barrier((held, r1, l1, before, after, rim))
    r2 = lax.ppermute(r1, "instance", ring("instance", 1))
    l2 = lax.ppermute(l1, "instance", ring("instance", -1))
    own_shift = lax.dynamic_slice_in_dim(rotor_shift, jnp.asarray(slots)[sector] * instances // sectors, 1)
    table = jnp.concatenate([own_shift, jnp.asarray(slots, jnp.int32)])
    ghosts = lax.all_to_all(turn_annulus(held, table, order), "sector", 0, 0, axis_index_groups=[order])
    ghosts = ghosts.reshape(rotor.shape)

    middle = jnp.zeros(flow.shape[:-1] + (LANE - 4,), flow.dtype)
    side = jnp.concatenate([after.swapaxes(3, 4), middle, before.swapaxes(3, 4)], -1)
    low = jnp.pad(jnp.where(radial == 0, 0.0, rim), ((0, 0),) * 3 + ((SUB - 2, 0), (0, 0)))
    high = jnp.pad(jnp.where(radial == 0, rim, 0.0), ((0, 0),) * 3 + ((0, SUB - 2), (0, 0)))
    jac = jacobians.reshape(-1) * (0.5 * PSEUDO_STEP)
    part = interior(flow, side, low, high, (r1, l1), jac)
    far = jnp.stack([row[3] * r2 + row[4] * l2 for row in SOURCE])
    part = part - (PSEUDO_STEP * FREQUENCY) * far
    axial = jacobians[2] * (0.5 * PSEUDO_STEP) + (4.0 * PSEUDO_STEP * DAMPING) * jnp.eye(variables)
    return add_ghosts(part, ghosts, rotor_shift, axial.reshape(-1))


def solution(mesh):
    return jax.shard_map(
        on_device,
        mesh=mesh,
        in_specs=(
            P("instance", None, None, "radial", "sector"),
            P("instance", None, None, "radial", "sector"),
            P(),
            P("instance"),
        ),
        out_specs=P("instance", None, None, "radial", "sector"),
        check_vma=False,
    )
```
